32 devices in a mesh: dp: 8 (over y, x, core), tensor: 4 (over z).
Axes of the slice: x: 2, y: 2, z: 4, core: 2. Of those that a mesh axis runs over, the one named last changes fastest.
Arguments:
- inputs: bfloat16 [3, 8192, 640], P(None, ('dp', 'tensor')), may hold values from -6 to 6
- grad_out: bfloat16 [3, 8192, 640], P(None, ('dp', 'tensor')), may hold values from -6 to 6
- masked: int32 [3, 8192], P(None, 'dp'), may hold values 0 or 1
- bucket: int32 [3, 8], P(None, 'dp'), may hold values from 0 to 2, as said below
- lengths: int32 [3, 32], P(None, 'dp'), may hold values from 1 to 1024, as said below
- first_gain: float32 [640], replicated, may hold values from 0.5 to 1.5
- first_shift: float32 [640], replicated, may hold values from -1.2 to 1.2
- second_gain: float32 [640], replicated, may hold values from 0.5 to 1.5
- second_shift: float32 [640], replicated, may hold values from -1.2 to 1.2
- qkv_weight: bfloat16 [3, 640, 640], P(None, 'dp', 'tensor'), may hold values from -0.25 to 0.25
- qkv_bias: float32 [3, 640], replicated, may hold values from -1.2 to 1.2
- out_weight: bfloat16 [640, 640], P('dp', 'tensor'), may hold values from -2 to 2
- out_bias: float32 [640], replicated, may hold values from -1.2 to 1.2
- up_weight: bfloat16 [640, 2560], P('dp', 'tensor'), may hold values from -0.25 to 0.25
- up_bias: float32 [2560], replicated, may hold values from -1.2 to 1.2
- down_weight: bfloat16 [640, 2560], P('dp', 'tensor'), may hold values from -0.125 to 0.125
- down_bias: float32 [640], replicated, may hold values from -1.2 to 1.2
Outputs:
- layer_out: bfloat16 [3, 8192, 640], P(None, ('dp', 'tensor'))
- grad_inputs: float32 [3, 8192, 640], P(None, ('dp', 'tensor'))
- grad_qkv_weight: float32 [3, 640, 640], P(None, 'dp', 'tensor')
- grad_out_weight: float32 [640, 640], P('dp', 'tensor')
- grad_up_weight: float32 [640, 2560], P('dp', 'tensor')
- grad_down_weight: float32 [640, 2560], P('dp', 'tensor')
- grad_first_gain: float32 [640], replicated
- grad_first_shift: float32 [640], replicated
- grad_second_gain: float32 [640], replicated
- grad_second_shift: float32 [640], replicated
- grad_qkv_bias: float32 [3, 640], replicated
- grad_out_bias: float32 [640], replicated
- grad_up_bias: float32 [2560], replicated
- grad_down_bias: float32 [640], replicated
The draws below stay inside these ranges and needn't reach their ends.
Inputs may be any that keep to these rules, and one draw needn't show every extreme that they name: Group r of micro-batch m holds sequences in slots of 1024 // 2**bucket[m, r] rows; in every micro-batch one group has 0 and another 2. `lengths`: entry r * 4 + s is the length of the sequence whose slot starts at row s * 256 of group r, where one starts there; other entries are not read. A length is at most its slot's width, and the first sequence of every group fills its slot.
All inputs are finite; a program needn't handle non-finite values. No bound on the sum of `masked` on one device may be relied on, other than what follows from the above.
Results may differ from the reference program's by a relative error of at most 0.015.
Values may be sent and summed in bfloat16 or wider, within the bound.
No kernel may reach another device: no remote copies, remote signals or barrier semaphores. Data moves between devices by JAX's collectives and lax.ppermute only.
A program may use at most 256 MiB of HBM per device.

```python
import jax
import jax.numpy as jnp
from jax import lax

D = 640
HEADS = 20
FF = 2560
HEAD_DIM = 32
MB = 3
GROUP = 1024
WINDOW = 1024
QUARTER = 256
SLOTS = 4
TOKENS = 8192
N_DP = 8


def bucket_table(key):
    code_table = jax.random.randint(jax.random.fold_in(key, 101), (MB, N_DP), 0, 3)
    first_pick = jax.random.randint(jax.random.fold_in(key, 102), (MB, 1), 0, N_DP)
    offset_pick = jax.random.randint(jax.random.fold_in(key, 103), (MB, 1), 1, N_DP)
    second_pick = (first_pick + offset_pick) % N_DP
    columns = jnp.arange(N_DP)[None, :]
    code_table = jnp.where(columns == first_pick, 0, code_table)
    code_table = jnp.where(columns == second_pick, 2, code_table)
    return code_table.astype(jnp.int32)


def draw_bucket(key, part):
    code_table = bucket_table(key)
    return code_table


def draw_lengths(key, part):
    code_table = bucket_table(key)
    key = jax.random.fold_in(key, 7)
    widths = jnp.int32(WINDOW) // jnp.left_shift(jnp.int32(1), code_table)
    random_bits = jax.random.randint(key, (MB, N_DP, SLOTS), 0, 1 << 20)
    length_table = 1 + random_bits % widths[:, :, None]
    leading = jnp.arange(SLOTS)[None, None, :] == 0
    length_table = jnp.where(leading, widths[:, :, None], length_table)
    return length_table.reshape(MB, N_DP * SLOTS).astype(jnp.int32)


def touch_ends(array, own_key, smallest, top_value):
    longest = array.shape.index(max(array.shape))
    spots = []
    for shift in (0, 1):
        where = [jax.random.randint(jax.random.fold_in(own_key, axis), (), 0, length) for axis, length in enumerate(array.shape)]
        where[longest] = (where[longest] + shift) % array.shape[longest]
        spots.append(tuple(where))
    return array.at[spots[0]].set(smallest).at[spots[1]].set(top_value)


def levels(key, shape, shards, smallest, high):
    def one(axis_at, shards_of):
        heights = jax.random.uniform(jax.random.fold_in(jax.random.fold_in(key, 6), axis_at), (shards_of,), jnp.float32, smallest / len(shards), high / len(shards))
        return jnp.repeat(jnp.exp(heights), shape[axis_at] // shards_of).reshape((-1,) + (1,) * (len(shape) - axis_at - 1))

    loudness = one(*shards[0])
    for cut in shards[1:]:
        loudness = loudness * one(*cut)
    return loudness


def normal_values(own_key, extent, scale, bound, split=(), held_as=jnp.bfloat16):
    array = jax.random.normal(own_key, extent, jnp.float32) * scale
    if len(split) > 0:
        array = levels(own_key, extent, split, -0.22, 0.18) * array
    return jnp.clip(array, min=-bound, max=bound).astype(held_as)


def setup_inputs(seed: int = 0) -> dict:
    arg_keys = jax.random.split(jax.random.key(seed), 18)
    return {
        "inputs": normal_values(arg_keys[0], (MB, TOKENS, D), 1.0, 6.0, ((1, 32),)),
        "grad_out": normal_values(arg_keys[1], (MB, TOKENS, D), 1.0, 6.0, ((1, 32),)),
        "masked": touch_ends((jax.random.randint(arg_keys[2], (MB, TOKENS), 0, 2) < 1).astype(jnp.int32), jax.random.fold_in(arg_keys[2], 1), 0, 1),
        "bucket": draw_bucket(jax.random.fold_in(arg_keys[17], 71), 0),
        "lengths": draw_lengths(jax.random.fold_in(arg_keys[17], 71), 0),
        "first_gain": jnp.clip(1.0 + 0.1 * jax.random.normal(arg_keys[5], (D,), jnp.float32), 0.5, 1.5),
        "first_shift": normal_values(arg_keys[6], (D,), 0.2, 1.2, (), jnp.float32),
        "second_gain": jnp.clip(1.0 + 0.1 * jax.random.normal(arg_keys[7], (D,), jnp.float32), 0.5, 1.5),
        "second_shift": normal_values(arg_keys[8], (D,), 0.2, 1.2, (), jnp.float32),
        "qkv_weight": normal_values(arg_keys[9], (3, D, D), D ** -0.5, 0.25, ((1, 8), (2, 4))),
        "qkv_bias": normal_values(arg_keys[10], (3, D), 0.2, 1.2, (), jnp.float32),
        "out_weight": normal_values(arg_keys[11], (D, D), (D // 64) ** -0.5, 2.0, ((0, 8), (1, 4))),
        "out_bias": normal_values(arg_keys[12], (D,), 0.2, 1.2, (), jnp.float32),
        "up_weight": normal_values(arg_keys[13], (D, FF), D ** -0.5, 0.25, ((0, 8), (1, 4))),
        "up_bias": normal_values(arg_keys[14], (FF,), 0.2, 1.2, (), jnp.float32),
        "down_weight": normal_values(arg_keys[15], (D, FF), FF ** -0.5, 0.125, ((0, 8), (1, 4))),
        "down_bias": normal_values(arg_keys[16], (D,), 0.2, 1.2, (), jnp.float32),
    }


@jax.custom_vjp
def low(v):
    return lax.optimization_barrier(v.astype(jnp.bfloat16)).astype(jnp.float32)

@jax.custom_vjp
def low_back(v):
    return v

def low_keep(v):
    return (low(v), None)

def low_pass(kept, grad):
    return (grad,)

def back_keep(v):
    return (v, None)

def back_low(kept, grad):
    return (low(grad),)
low.defvjp(low_keep, low_pass)
low_back.defvjp(back_keep, back_low)
HIGH = lax.Precision.HIGHEST

def layer_norm(values, gain_row, shift_row):
    average = lax.optimization_barrier(jnp.mean(values, -1, keepdims=True))
    centred = values - average
    spread = lax.optimization_barrier(jnp.mean(centred * centred, -1, keepdims=True))
    return centred * lax.rsqrt(spread + 1e-05) * gain_row + shift_row

def layout(bucket_code, slot_lengths, row_total):
    block_rows = jnp.arange(row_total, dtype=jnp.int32)
    seq_width = jnp.int32(WINDOW) // jnp.left_shift(jnp.int32(1), bucket_code.astype(jnp.int32))
    position = block_rows % seq_width
    sequence = block_rows // seq_width
    slot_index = (block_rows - position) // QUARTER
    matches = slot_index[:, None] == jnp.arange(slot_lengths.shape[0], dtype=jnp.int32)[None, :]
    length_row = lax.optimization_barrier(jnp.sum(jnp.where(matches, slot_lengths[None, :], 0), axis=1)).astype(jnp.int32)
    return (position, sequence, length_row)

def rotary(values, position):
    halfway = values.shape[-1] // 2
    frequency = 1.0 / 10000.0 ** (jnp.arange(halfway, dtype=jnp.float32) * 2.0 / values.shape[-1])
    angles = position.astype(jnp.float32)[:, None] * frequency[None, :]
    angles = jnp.concatenate([angles, angles], -1)
    turned = jnp.concatenate([-values[..., halfway:], values[..., :halfway]], -1)
    return values * jnp.cos(angles)[:, None, :] + turned * jnp.sin(angles)[:, None, :]

def group_forward(params, block_rows, bucket_code, slot_lengths):
    first_gain, first_shift, second_gain, second_shift, qkv_weight, qkv_bias, out_weight, out_bias, up_weight, up_bias, down_weight, down_bias = params
    row_total = block_rows.shape[0]
    position, sequence, length_row = layout(bucket_code, slot_lengths, row_total)
    first_normed = low(layer_norm(block_rows, first_gain, first_shift))
    qkv_rows = low_back(jnp.einsum('gd,sdc->sgc', first_normed, qkv_weight, precision=HIGH) + qkv_bias[:, None, :])
    pieces = qkv_rows.reshape(3, row_total, HEADS, HEAD_DIM)
    queries = low(rotary(pieces[0], position) * HEAD_DIM ** (-0.5))
    keys_low = low(rotary(pieces[1], position))
    values_low = low(pieces[2])
    windows = row_total // WINDOW
    window_shape = (windows, WINDOW, HEADS, HEAD_DIM)
    scores = low_back(jnp.einsum('nqhe,nkhe->nhqk', queries.reshape(window_shape), keys_low.reshape(window_shape), precision=HIGH))
    seq_blocks = sequence.reshape(windows, WINDOW)
    pos_blocks = position.reshape(windows, WINDOW)
    len_blocks = length_row.reshape(windows, WINDOW)
    visible = (seq_blocks[:, :, None] == seq_blocks[:, None, :]) & (pos_blocks[:, None, :] < len_blocks[:, None, :])
    scores = jnp.where(visible[:, None], scores, -1e+30)
    highest = lax.optimization_barrier(jnp.max(scores, -1, keepdims=True))
    weights = jnp.exp(scores - highest)
    probability = low(weights / lax.optimization_barrier(jnp.sum(weights, -1, keepdims=True)))
    attended = jnp.einsum('nhqk,nkhe->nqhe', probability, values_low.reshape(window_shape), precision=HIGH)
    attended = low(low_back(attended.reshape(row_total, D)))
    mixed_rows = low_back(jnp.dot(attended, out_weight.T, precision=HIGH, preferred_element_type=jnp.float32))
    residual = block_rows + mixed_rows + out_bias
    second_normed = low(layer_norm(residual, second_gain, second_shift))
    up_pre = low_back(jnp.dot(second_normed, up_weight, precision=HIGH, preferred_element_type=jnp.float32) + up_bias)
    hidden = low(jax.nn.gelu(up_pre, approximate=False))
    down_rows = low_back(jnp.dot(hidden, down_weight.T, precision=HIGH, preferred_element_type=jnp.float32))
    return residual + down_rows + down_bias

def reference(inputs, grad_out, masked, bucket, lengths, first_gain, first_shift, second_gain, second_shift, qkv_weight, qkv_bias, out_weight, out_bias, up_weight, up_bias, down_weight, down_bias):
    params = tuple((item.astype(jnp.float32) for item in (first_gain, first_shift, second_gain, second_shift, qkv_weight, qkv_bias, out_weight, out_bias, up_weight, up_bias, down_weight, down_bias)))
    groups = MB * N_DP
    block_rows = inputs.astype(jnp.float32).reshape(groups, GROUP, D)
    bucket_codes = bucket.reshape(groups).astype(jnp.int32)
    slot_lengths = lengths.reshape(groups, SLOTS).astype(jnp.int32)
    picked = masked.reshape(groups, GROUP).astype(jnp.int32)
    cotangent_rows = grad_out.astype(jnp.float32).reshape(groups, GROUP, D)

    def cotangent(bucket_code, slot_row, picked_row, grad_rows):
        position, sequence, length_row = layout(bucket_code, slot_row, GROUP)
        counted = jnp.where(position < length_row, picked_row, 0).astype(jnp.float32)
        factor = 3.0 * GROUP / 8.0 / jnp.maximum(jnp.sum(counted), 1.0)
        return grad_rows * (counted * factor)[:, None]
    cotangents = jax.vmap(cotangent)(bucket_codes, slot_lengths, picked, cotangent_rows)
    checked = jax.checkpoint(group_forward)

    def run(param_set, rows_all):

        def scan_step(carry, members):
            return (carry, checked(param_set, members[0], members[1], members[2]))
        carry, results = lax.scan(scan_step, jnp.float32(0.0), (rows_all, bucket_codes, slot_lengths))
        return results
    results, pullback = jax.vjp(run, params, block_rows)
    grad_params, grad_rows = pullback(cotangents)
    g_first_gain, g_first_shift, g_second_gain, g_second_shift, g_qkv_weight, g_qkv_bias, g_out_weight, g_out_bias, g_up_weight, g_up_bias, g_down_weight, g_down_bias = grad_params
    layer_out = results.reshape(MB, TOKENS, D).astype(jnp.bfloat16)
    grad_inputs = grad_rows.reshape(MB, TOKENS, D)
    return (layer_out, grad_inputs, g_qkv_weight, g_out_weight, g_up_weight, g_down_weight, g_first_gain, g_first_shift, g_second_gain, g_second_shift, g_qkv_bias, g_out_bias, g_up_bias, g_down_bias)
```

```python
import functools

import jax
import jax.numpy as jnp
import numpy as np
from jax import lax
from jax.experimental import pallas as pl
from jax.experimental.pallas import tpu as pltpu
from jax.sharding import PartitionSpec as P

HEAD_DIM = 32
LANES = 128
PACK = LANES // HEAD_DIM
BLOCK = 256
VMEM = 60 * 2**20
BF = jnp.bfloat16
F32 = jnp.float32
NN = (((1,), (0,)), ((), ()))
NT = (((1,), (1,)), ((), ()))
TN = (((0,), (0,)), ((), ()))


def dot(left, right, dims=NN):
    return lax.dot_general(left, right, dims, preferred_element_type=F32)


def params():
    return pltpu.CompilerParams(vmem_limit_bytes=VMEM)


def cost(flops, moved, transcendentals=0):
    return pl.CostEstimate(flops=flops, bytes_accessed=moved, transcendentals=transcendentals)


def whole(shape):
    return pl.BlockSpec(shape, lambda *_: (0,) * len(shape))


def norm(values):
    centred = values - jnp.mean(values, -1, keepdims=True)
    factor = lax.rsqrt(jnp.mean(centred * centred, -1, keepdims=True) + 1e-05)
    return centred * factor, factor


def norm_back(gradient, unit_rows, factor, gain_row):
    scaled = gradient * gain_row
    return factor * (
        scaled
        - jnp.mean(scaled, -1, keepdims=True)
        - unit_rows * jnp.mean(scaled * unit_rows, -1, keepdims=True)
    )


def rotary_tables(rows):
    halfway = HEAD_DIM // 2
    frequency = (1.0 / 10000.0 ** (np.arange(halfway, dtype=np.float32) * 2.0 / HEAD_DIM)).astype(np.float32)
    angles = np.arange(rows, dtype=np.float32)[:, None] * frequency[None, :]
    cosine = np.tile(np.cos(angles), (1, LANES // halfway)).astype(np.float32)
    sine = np.sin(angles)
    sine = np.tile(np.concatenate([-sine, sine], 1), (1, PACK)).astype(np.float32)
    return jnp.asarray(cosine), jnp.asarray(sine)


def swap_halves(values):
    halfway = HEAD_DIM // 2
    lane = lax.broadcasted_iota(jnp.int32, values.shape, 1)
    return jnp.where(
        lane % HEAD_DIM < halfway,
        pltpu.roll(values, LANES - halfway, 1),
        pltpu.roll(values, halfway, 1),
    )


def project_kernel(place_ref, *refs, parts, width):
    blocks = refs[:parts]
    gain_ref, shift_ref, weight_ref, bias_ref, cos_ref, sin_ref, x_ref, normed_ref, qkv_ref = refs[parts:]
    rows = blocks[0].shape[0]
    slot = lax.shift_right_logical(jnp.int32(rows * parts), place_ref[0])
    for part in range(parts):
        start = pl.multiple_of(place_ref[1 + part], rows)
        here = pl.ds(start, rows)
        x = blocks[part][...]
        x_ref[here, :] = x
        unit_rows, _ = norm(x.astype(F32))
        normed = (unit_rows * gain_ref[...] + shift_ref[...]).astype(BF)
        normed_ref[here, :] = normed
        at = pl.ds(pl.multiple_of(lax.rem(start, slot), rows), rows)
        cosine, sine = cos_ref[at, :], sin_ref[at, :]
        for s in range(3):
            rows_out = dot(normed, weight_ref[:, s * width : (s + 1) * width])
            rows_out = rows_out + bias_ref[:, s * width : (s + 1) * width]
            if s == 2:
                qkv_ref[here, s * width : (s + 1) * width] = rows_out.astype(BF)
                continue
            for tile in range(width // LANES):
                piece = rows_out[:, tile * LANES : (tile + 1) * LANES]
                piece = piece * cosine + swap_halves(piece) * sine
                if s == 0:
                    piece = piece * HEAD_DIM ** (-0.5)
                column = s * width + tile * LANES
                qkv_ref[here, column : column + LANES] = piece.astype(BF)


def project(place, blocks, gain, shift, weight, bias, cosine, sine):
    parts = len(blocks)
    rows, width = blocks[0].shape
    total = rows * parts
    return pl.pallas_call(
        functools.partial(project_kernel, parts=parts, width=width),
        in_specs=[pl.BlockSpec(memory_space=pltpu.SMEM)] + [pl.BlockSpec(memory_space=pltpu.VMEM)] * (parts + 6),
        out_specs=[pl.BlockSpec(memory_space=pltpu.VMEM)] * 3,
        out_shape=[
            jax.ShapeDtypeStruct((total, width), BF),
            jax.ShapeDtypeStruct((total, width), BF),
            jax.ShapeDtypeStruct((total, 3 * width), BF),
        ],
        compiler_params=params(),
        cost_estimate=cost(6 * total * width * width, 12 * total * width),
        name="project",
    )(place, *blocks, gain, shift, weight, bias, cosine, sine)


def by_bucket(bucket, total, lens_ref, body):
    for code in range(3):
        count = 1 << code
        width = total // count
        step = 4 // count

        @pl.when(bucket == code)
        def _(count=count, width=width, step=step):
            if count == 1:
                body(0, width, lens_ref[0])
            else:

                @pl.loop(0, count)
                def _(index):
                    body(pl.multiple_of(index * width, width), width, lens_ref[step * index])


def attend_kernel(place_ref, lens_ref, q_ref, k_ref, v_ref, out_ref, log_ref):
    total = q_ref.shape[0]
    lane = lax.broadcasted_iota(jnp.int32, (1, LANES), 1)
    area = lane // HEAD_DIM
    sub = lane % HEAD_DIM

    def sequence(first, width, length):
        keys, values = k_ref[pl.ds(first, width), :], v_ref[pl.ds(first, width), :]
        position = lax.broadcasted_iota(jnp.int32, (width, 1), 0)
        hidden = jnp.where(position < length, 0.0, -1e30).astype(BF)
        for start in range(0, width, BLOCK):
            here = pl.ds(first + start, BLOCK)
            queries = q_ref[here, :]
            total_rows, highs = None, []
            for head in range(PACK):
                own = area == head
                extra = (area == (head + 1) % PACK) & (sub == 0)
                q_one = jnp.where(own, queries, jnp.where(extra, BF(1), BF(0)))
                k_one = jnp.where(extra, jnp.broadcast_to(hidden, keys.shape), keys)
                scores = dot(q_one, k_one, NT)
                high = jnp.max(scores, 1, keepdims=True)
                weights = jnp.exp(scores - high).astype(BF)
                v_one = jnp.concatenate(
                    [
                        jnp.where(own, values, BF(0)),
                        jnp.broadcast_to(jnp.where(own, BF(1), BF(0)), values.shape),
                    ],
                    1,
                )
                term = dot(weights, v_one)
                total_rows = term if total_rows is None else total_rows + term
                highs.append(high)
            high = highs[PACK - 1]
            for head in range(PACK - 1):
                high = jnp.where(area == head, highs[head], high)
            summed = total_rows[:, LANES:]
            out_ref[here, :] = (total_rows[:, :LANES] / summed).astype(BF)
            log_ref[here, :] = high + jnp.log(summed)

    by_bucket(place_ref[0], total, lens_ref, sequence)


def attend(place, lens, qkv):
    total = qkv.shape[0]
    tiles = qkv.shape[1] // 3 // LANES
    scalar = pl.BlockSpec(memory_space=pltpu.SMEM)

    def tile(which):
        return pl.BlockSpec((total, LANES), lambda j: (0, which * tiles + j))

    return pl.pallas_call(
        attend_kernel,
        grid=(tiles,),
        in_specs=[scalar, scalar, tile(0), tile(1), tile(2)],
        out_specs=[tile(0), tile(0)],
        out_shape=[
            jax.ShapeDtypeStruct((total, tiles * LANES), BF),
            jax.ShapeDtypeStruct((total, tiles * LANES), F32),
        ],
        compiler_params=params(),
        cost_estimate=cost(
            12 * tiles * PACK * total * total * 256, 12 * total * tiles * LANES, tiles * PACK * total * total
        ),
        name="attend",
    )(place, lens, qkv, qkv, qkv)


def split3(values):
    first = values.astype(BF)
    rest = values - first.astype(F32)
    second = rest.astype(BF)
    return first, second, (rest - second.astype(F32)).astype(BF)


def attend_back_kernel(
    place_ref, lens_ref, q_ref, k_ref, v_ref, out_ref, grad_ref, log_ref, cos_ref, sin_ref,
    dq_ref, dk_ref, dv_ref, q_extra, g_extra, dq_total, dk_total,
):
    total = q_ref.shape[0]
    lane = lax.broadcasted_iota(jnp.int32, (1, LANES), 1)
    area = lane // HEAD_DIM
    sub = lane % HEAD_DIM
    first, second, third = split3(-pltpu.roll(log_ref[...], HEAD_DIM, 1))
    q_extra[...] = jnp.where(
        sub == 0, first, jnp.where(sub == 1, second, jnp.where(sub == 2, third, jnp.where(sub == 3, BF(1), BF(0))))
    )
    product = grad_ref[...].astype(F32) * out_ref[...].astype(F32)
    row_area = lax.broadcasted_iota(jnp.int32, (LANES, LANES), 0) // HEAD_DIM
    column_area = lax.broadcasted_iota(jnp.int32, (LANES, LANES), 1) // HEAD_DIM
    spread = jnp.where((row_area + 1) % PACK == column_area, 1.0, 0.0).astype(BF)
    delta = sum(dot(piece, spread) for piece in split3(product))
    first, second, third = split3(-delta)
    g_extra[...] = jnp.where(sub == 0, first, jnp.where(sub == 1, second, jnp.where(sub == 2, third, BF(0))))

    def sequence(begin, width, length):
        keys, values = k_ref[pl.ds(begin, width), :], v_ref[pl.ds(begin, width), :]
        position = lax.broadcasted_iota(jnp.int32, (width, 1), 0)
        hidden = jnp.where(position < length, 0.0, -1e30).astype(BF)
        k_extra = jnp.where(
            sub < 3, BF(1), jnp.where(sub == 3, jnp.broadcast_to(hidden, keys.shape), BF(0))
        )
        v_extra = jnp.broadcast_to(jnp.where(sub < 3, BF(1), BF(0)), values.shape)
        dv = jnp.zeros((width, LANES), F32)
        dk = jnp.zeros((width, LANES), F32)
        for start in range(0, width, BLOCK):
            here = pl.ds(begin + start, BLOCK)
            queries, grads = q_ref[here, :], grad_ref[here, :]
            q_more, g_more = q_extra[here, :], g_extra[here, :]
            dq = None
            for head in range(PACK):
                own, after = area == head, area == (head + 1) % PACK
                q_own, g_own = jnp.where(own, queries, BF(0)), jnp.where(own, grads, BF(0))
                k_one, v_one = jnp.where(own, keys, k_extra), jnp.where(own, values, v_extra)
                prob = jnp.exp(dot(k_one, jnp.where(after, q_more, q_own), NT))
                grad_prob = dot(v_one, jnp.where(after, g_more, g_own), NT)
                grad_scores = (prob * grad_prob).astype(BF)
                dv = dv + dot(prob.astype(BF), g_own)
                dk = dk + dot(grad_scores, q_own)
                term = dot(jnp.where(own, keys, BF(0)), grad_scores, TN)
                dq = term if dq is None else dq + term
            dq_total[here, :] = dq.T
        dv_ref[pl.ds(begin, width), :] = dv.astype(BF)
        dk_total[pl.ds(begin, width), :] = dk

    by_bucket(place_ref[0], total, lens_ref, sequence)
    slot = lax.shift_right_logical(jnp.int32(total), place_ref[0])
    for start in range(0, total, BLOCK):
        here = pl.ds(start, BLOCK)
        at = pl.ds(pl.multiple_of(lax.rem(jnp.int32(start), slot), BLOCK), BLOCK)
        cosine, sine = cos_ref[at, :], sin_ref[at, :]
        dq, dk = dq_total[here, :], dk_total[here, :]
        dq_ref[here, :] = ((dq * cosine - swap_halves(dq) * sine) * HEAD_DIM ** (-0.5)).astype(BF)
        dk_ref[here, :] = (dk * cosine - swap_halves(dk) * sine).astype(BF)


def attend_back(place, lens, qkv, attended, grad, log_total, cosine, sine):
    total = qkv.shape[0]
    tiles = qkv.shape[1] // 3 // LANES
    scalar = pl.BlockSpec(memory_space=pltpu.SMEM)

    def tile(which):
        return pl.BlockSpec((total, LANES), lambda j: (0, which * tiles + j))

    return pl.pallas_call(
        attend_back_kernel,
        grid=(tiles,),
        in_specs=[scalar, scalar, tile(0), tile(1), tile(2), tile(0), tile(0), tile(0)]
        + [whole((total, LANES))] * 2,
        out_specs=[tile(0)] * 3,
        out_shape=[jax.ShapeDtypeStruct((total, tiles * LANES), BF)] * 3,
        scratch_shapes=[pltpu.VMEM((total, LANES), BF)] * 2 + [pltpu.VMEM((total, LANES), F32)] * 2,
        compiler_params=params(),
        cost_estimate=cost(
            24 * tiles * PACK * total * total * 256, 20 * total * tiles * LANES, tiles * PACK * total * total
        ),
        name="attend_back",
    )(place, lens, qkv, qkv, qkv, attended, grad, log_total, cosine, sine)


def column_sums(values):
    return jnp.sum(values, 0, keepdims=True)


def feed_kernel(
    place_ref, x_ref, att_ref, grad_ref, weight_ref, gain_ref, shift_ref, out_bias_ref, up_bias_ref, down_bias_ref,
    up_ref, down_ref, mix_ref,
    layer_ref, residual_ref, grad_att_ref, sums_ref, grads_ref,
    normed, tops, mixes, atts, hidden, ups, *, row_steps, chunks,
):
    step = pl.program_id(0)
    rows, width = x_ref.shape

    @pl.when(step == 0)
    def _():
        sums_ref[...] = jnp.zeros_like(sums_ref)

    @pl.when(step < row_steps)
    def _():
        here = pl.ds(pl.multiple_of(step * rows, rows), rows)
        attended = att_ref[...]
        residual = x_ref[...].astype(F32) + dot(attended, mix_ref[...], NT) + out_bias_ref[...]
        unit_rows, factor = norm(residual)
        gain = gain_ref[...]
        second = (unit_rows * gain + shift_ref[...]).astype(BF)
        top = grad_ref[0].astype(F32) * weight_ref[...]
        top_low = top.astype(BF)
        normed[here, :] = second
        tops[here, :] = top_low
        atts[here, :] = attended
        below = jnp.zeros((rows, width), F32)
        grad_second = jnp.zeros((rows, width), F32)
        for chunk in range(chunks):
            columns = slice(chunk * width, (chunk + 1) * width)
            up_weight, down_weight = up_ref[:, columns], down_ref[:, columns]
            up = dot(second, up_weight) + up_bias_ref[:, columns]
            share = 0.5 * (1.0 + lax.erf(up * 0.7071067811865476))
            slope = share + up * jnp.exp(-0.5 * up * up) * 0.3989422804014327
            low = (up * share).astype(BF)
            hidden[here, columns] = low
            below = below + dot(low, down_weight, NT)
            grad_up = (dot(top_low, down_weight) * slope).astype(BF)
            ups[here, columns] = grad_up
            sums_ref[4 + chunk : 5 + chunk, :] += column_sums(grad_up.astype(F32))
            grad_second = grad_second + dot(grad_up, up_weight, NT)
        layer_ref[...] = (residual + below + down_bias_ref[...]).astype(BF)
        grad_residual = top + norm_back(grad_second, unit_rows, factor, gain)
        residual_ref[...] = grad_residual
        mixed = grad_residual.astype(BF)
        mixes[here, :] = mixed
        grad_att_ref[...] = dot(mixed, mix_ref[...]).astype(BF)
        sums_ref[0:1, :] += column_sums(grad_second * unit_rows)
        sums_ref[1:2, :] += column_sums(grad_second)
        sums_ref[2:3, :] += column_sums(grad_residual)
        sums_ref[3:4, :] += column_sums(top)

    for chunk in range(chunks):
        columns = slice(chunk * width, (chunk + 1) * width)

        @pl.when(step == row_steps + chunk)
        def _(columns=columns):
            grads_ref[...] = dot(normed[...], ups[:, columns], TN).astype(BF)

        @pl.when(step == row_steps + chunks + chunk)
        def _(columns=columns):
            grads_ref[...] = dot(tops[...], hidden[:, columns], TN).astype(BF)

    @pl.when(step == row_steps + 2 * chunks)
    def _():
        grads_ref[...] = dot(mixes[...], atts[...], TN).astype(BF)


def feed(place, x, attended, grad_blocks, row_weight, gain, shift, out_bias, up_bias, down_bias, weights):
    total, width = x.shape
    parts, rows = grad_blocks.shape[:2]
    hidden_width = up_bias.shape[1]
    chunks = hidden_width // width

    def last(i):
        return jnp.minimum(i, parts - 1)

    row = pl.BlockSpec((rows, width), lambda i, place: (last(i), 0))
    grid_spec = pltpu.PrefetchScalarGridSpec(
        num_scalar_prefetch=1,
        grid=(parts + 2 * chunks + 1,),
        in_specs=[
            row,
            row,
            pl.BlockSpec((1, rows, width), lambda i, place: (place[1 + last(i)] // rows, 0, 0)),
            pl.BlockSpec((rows, 1), lambda i, place: (last(i), 0)),
            whole((1, width)),
            whole((1, width)),
            whole((1, width)),
            whole((1, hidden_width)),
            whole((1, width)),
            pl.BlockSpec((width, hidden_width), lambda i, place: (0, 0), pipeline_mode=pl.Buffered(1)),
            pl.BlockSpec((width, hidden_width), lambda i, place: (0, 1), pipeline_mode=pl.Buffered(1)),
            pl.BlockSpec((width, width), lambda i, place: (0, 2 * chunks), pipeline_mode=pl.Buffered(1)),
        ],
        out_specs=[
            row,
            row,
            row,
            whole((16, width)),
            pl.BlockSpec((width, width), lambda i, place: (0, jnp.maximum(i - parts, 0))),
        ],
        scratch_shapes=[pltpu.VMEM((total, width), BF)] * 4 + [pltpu.VMEM((total, hidden_width), BF)] * 2,
    )
    return pl.pallas_call(
        functools.partial(feed_kernel, row_steps=parts, chunks=chunks),
        grid_spec=grid_spec,
        out_shape=[
            jax.ShapeDtypeStruct((total, width), BF),
            jax.ShapeDtypeStruct((total, width), F32),
            jax.ShapeDtypeStruct((total, width), BF),
            jax.ShapeDtypeStruct((16, width), F32),
            jax.ShapeDtypeStruct((width, (2 * chunks + 1) * width), BF),
        ],
        compiler_params=params(),
        cost_estimate=cost(6 * total * width * width * (2 * chunks + 1), 24 * width * hidden_width),
        name="feed",
    )(place, x, attended, grad_blocks, row_weight, gain, shift, out_bias, up_bias, down_bias, weights, weights, weights)


def project_grads_kernel(normed_ref, q_ref, k_ref, v_ref, out_ref, sums_ref):
    for s, ref in enumerate((q_ref, k_ref, v_ref)):

        @pl.when(pl.program_id(0) == s)
        def _(s=s, ref=ref):
            grads = ref[...]
            out_ref[...] = dot(normed_ref[...], grads, TN).astype(BF)
            sums_ref[s : s + 1, :] = column_sums(grads.astype(F32))


def project_grads(normed, grads):
    total, width = normed.shape
    return pl.pallas_call(
        project_grads_kernel,
        grid=(3,),
        in_specs=[whole((total, width))] * 4,
        out_specs=[pl.BlockSpec((width, width), lambda i: (0, i)), whole((8, width))],
        out_shape=[jax.ShapeDtypeStruct((width, 3 * width), BF), jax.ShapeDtypeStruct((8, width), F32)],
        compiler_params=params(),
        cost_estimate=cost(6 * total * width * width, 14 * total * width),
        name="project_grads",
    )(normed, *grads)


def project_back_kernel(q_ref, k_ref, v_ref, weight_ref, x_ref, residual_ref, gain_ref, out_ref, sums_ref):
    width = x_ref.shape[1]

    @pl.when(pl.program_id(0) == 0)
    def _():
        sums_ref[...] = jnp.zeros_like(sums_ref)

    grad_first = sum(
        dot(ref[...], weight_ref[:, s * width : (s + 1) * width], NT) for s, ref in enumerate((q_ref, k_ref, v_ref))
    )
    unit_rows, factor = norm(x_ref[...].astype(F32))
    out_ref[...] = (residual_ref[...] + norm_back(grad_first, unit_rows, factor, gain_ref[...])).astype(BF)
    sums_ref[0:1, :] += column_sums(grad_first * unit_rows)
    sums_ref[1:2, :] += column_sums(grad_first)


def project_back(grads, weight, x, grad_residual, gain):
    total, width = x.shape
    row = pl.BlockSpec((BLOCK, width), lambda i: (i, 0))
    return pl.pallas_call(
        project_back_kernel,
        grid=(total // BLOCK,),
        in_specs=[row, row, row, whole((width, 3 * width)), row, row, whole((1, width))],
        out_specs=[row, whole((8, width))],
        out_shape=[jax.ShapeDtypeStruct((total, width), BF), jax.ShapeDtypeStruct((8, width), F32)],
        compiler_params=params(),
        cost_estimate=cost(6 * total * width * width, 16 * total * width),
        name="project_back",
    )(*grads, weight, x, grad_residual, gain)


def shards(
    inputs,
    grad_out,
    masked,
    bucket,
    lengths,
    first_gain,
    first_shift,
    second_gain,
    second_shift,
    qkv_weight,
    qkv_bias,
    out_weight,
    out_bias,
    up_weight,
    up_bias,
    down_weight,
    down_bias,
):
    parts = lax.axis_size("tensor")
    dp_parts = lax.axis_size("dp")
    here = lax.axis_index("tensor")
    dp_here = lax.axis_index("dp")
    micro_total, rows, width = inputs.shape
    total = rows * parts
    assert micro_total <= parts
    spare = parts - micro_total
    first = (dp_here % 2) * spare
    micro = here - first
    working = (micro >= 0) & (micro < micro_total)
    micro_at = jnp.clip(micro, 0, micro_total - 1)

    def pairs(shift, towards):
        out = []
        for r in range(dp_parts):
            for t in range(parts):
                u = (t + shift) % parts
                owner = (u if towards else t) - (r % 2) * spare
                if 0 <= owner < micro_total:
                    out.append((r * parts + t, r * parts + u))
        return out

    def collect(array):
        blocks = [lax.dynamic_index_in_dim(array, micro_at, 0, False)]
        for shift in range(1, parts):
            target = lax.rem(here + shift, parts)
            sent = lax.dynamic_index_in_dim(array, jnp.clip(target - first, 0, micro_total - 1), 0, False)
            blocks.append(lax.ppermute(sent, ("dp", "tensor"), pairs(shift, True)))
        return blocks

    def give_back(array):
        split = array.reshape(parts, rows, width)
        blocks = [lax.dynamic_index_in_dim(split, here, 0, False)]
        for shift in range(1, parts):
            sent = lax.dynamic_index_in_dim(split, lax.rem(here + shift, parts), 0, False)
            blocks.append(lax.ppermute(sent, ("dp", "tensor"), pairs(shift, False)))
        blocks = jnp.stack(blocks)
        return jnp.stack(
            [
                lax.dynamic_index_in_dim(blocks, lax.rem(here - first - m + parts, parts), 0, False)
                for m in range(micro_total)
            ]
        )

    def sum_everywhere(values):
        for axis, size in (("dp", dp_parts), ("tensor", parts)):
            bit = 1
            while bit < size:
                values = values + lax.ppermute(values, axis, [(i, i ^ bit) for i in range(size)])
                bit *= 2
        return values

    rows_w = qkv_weight.shape[1]
    attn = lax.all_gather(qkv_weight, "tensor", axis=0)
    attn = attn.transpose(2, 1, 0, 3).reshape(rows_w, 3 * width)
    attn = lax.all_gather(attn, "dp", axis=0, tiled=True)
    rest = jnp.concatenate([up_weight, down_weight, out_weight], 1)
    cols_ffn, cols_attn = up_weight.shape[1], out_weight.shape[1]
    rest = lax.all_gather(rest, "tensor", axis=0)
    rest = jnp.concatenate(
        [
            rest[:, :, :cols_ffn].transpose(1, 0, 2).reshape(rows_w, -1),
            rest[:, :, cols_ffn : 2 * cols_ffn].transpose(1, 0, 2).reshape(rows_w, -1),
            rest[:, :, 2 * cols_ffn :].transpose(1, 0, 2).reshape(rows_w, -1),
        ],
        1,
    )
    rest = lax.all_gather(rest, "dp", axis=0, tiled=True)

    code = jnp.where(working, lax.dynamic_index_in_dim(bucket, micro_at, 0, False)[0], 2).astype(jnp.int32)
    lens = lax.dynamic_index_in_dim(lengths, micro_at, 0, False)
    chosen = lax.dynamic_index_in_dim(masked, micro_at, 0, False)
    sources = lax.rem(here - jnp.arange(parts, dtype=jnp.int32) + parts, parts)
    place = jnp.concatenate([code[None], sources * rows]).astype(jnp.int32)
    row_ids = jnp.arange(total, dtype=jnp.int32)
    position = row_ids % (jnp.int32(total) // jnp.left_shift(jnp.int32(1), code))
    slot = (row_ids - position) // (total // 4)
    length_row = jnp.sum(jnp.where(slot[:, None] == jnp.arange(4)[None, :], lens[None, :], 0), 1)
    counted = jnp.where((position < length_row) & working, chosen, 0).astype(F32)
    row_weight = counted * (3.0 * total / 8.0 / jnp.maximum(jnp.sum(counted), 1.0))

    cosine, sine = rotary_tables(total)
    blocks = collect(inputs)
    grad_blocks = collect(grad_out)
    x, first_normed, qkv = project(
        place, blocks, first_gain[None], first_shift[None], attn, qkv_bias.reshape(1, -1), cosine, sine
    )
    attended, log_total = attend(place, lens, qkv)
    layer, grad_residual, grad_attended, feed_sums, feed_grads = feed(
        place, x, attended, jnp.stack(grad_blocks), row_weight[:, None], second_gain[None], second_shift[None],
        out_bias[None], up_bias[None], down_bias[None], rest,
    )
    layer_out = give_back(layer)
    feed_grads = lax.psum_scatter(feed_grads, "dp", scatter_dimension=0, tiled=True)
    wide = 2 * cols_ffn * parts
    feed_grads = jnp.concatenate(
        [
            feed_grads[:, : wide // 2].reshape(rows_w, parts, cols_ffn),
            feed_grads[:, wide // 2 : wide].reshape(rows_w, parts, cols_ffn),
            feed_grads[:, wide:].reshape(rows_w, parts, cols_attn),
        ],
        2,
    ).transpose(1, 0, 2)
    feed_grads = lax.psum_scatter(feed_grads, "tensor", scatter_dimension=0, tiled=False).astype(F32)
    grads = attend_back(place, lens, qkv, attended, grad_attended, log_total, cosine, sine)
    attn_grads, bias_sums = project_grads(first_normed, grads)
    grad_in, first_sums = project_back(grads, attn, x, grad_residual, first_gain[None])
    grad_inputs = give_back(grad_in).astype(F32)
    attn_grads = lax.psum_scatter(attn_grads, "dp", scatter_dimension=0, tiled=True)
    attn_grads = attn_grads.reshape(rows_w, 3, parts, cols_attn).transpose(2, 1, 0, 3)
    attn_grads = lax.psum_scatter(attn_grads, "tensor", scatter_dimension=0, tiled=False).astype(F32)
    feed_sums = sum_everywhere(feed_sums)
    late_sums = sum_everywhere(jnp.concatenate([bias_sums[:3], first_sums[:2]]))
    return (
        layer_out,
        grad_inputs,
        attn_grads,
        feed_grads[:, 2 * cols_ffn :],
        feed_grads[:, :cols_ffn],
        feed_grads[:, cols_ffn : 2 * cols_ffn],
        late_sums[3],
        late_sums[4],
        feed_sums[0],
        feed_sums[1],
        late_sums[:3],
        feed_sums[2],
        feed_sums[4 : 4 + up_bias.shape[0] // width].reshape(-1),
        feed_sums[3],
    )


def solution(mesh):
    placed = (
        P(None, ("dp", "tensor"), None),
        P(None, ("dp", "tensor"), None),
        P(None, "dp"),
        P(None, "dp"),
        P(None, "dp"),
        P(),
        P(),
        P(),
        P(),
        P(None, "dp", "tensor"),
        P(),
        P("dp", "tensor"),
        P(),
        P("dp", "tensor"),
        P(),
        P("dp", "tensor"),
        P(),
    )
    return jax.shard_map(
        shards,
        mesh=mesh,
        in_specs=placed,
        out_specs=(
            P(None, ("dp", "tensor"), None),
            P(None, ("dp", "tensor"), None),
            P(None, "dp", "tensor"),
            P("dp", "tensor"),
            P("dp", "tensor"),
            P("dp", "tensor"),
            P(),
            P(),
            P(),
            P(),
            P(),
            P(),
            P(),
            P(),
        ),
        check_vma=False,
    )
```

```python
import functools

import jax
import jax.numpy as jnp
import numpy as np
from jax import lax
from jax.experimental import pallas as pl
from jax.experimental.pallas import tpu as pltpu
from jax.sharding import PartitionSpec as P

HEAD_DIM = 32
LANES = 128
PACK = LANES // HEAD_DIM
BLOCK = 256
VMEM = 60 * 2**20
BF = jnp.bfloat16
F32 = jnp.float32
NN = (((1,), (0,)), ((), ()))
NT = (((1,), (1,)), ((), ()))
TN = (((0,), (0,)), ((), ()))


def dot(left, right, dims=NN):
    return lax.dot_general(left, right, dims, preferred_element_type=F32)


def params():
    return pltpu.CompilerParams(vmem_limit_bytes=VMEM)


def cost(flops, moved, transcendentals=0):
    return pl.CostEstimate(flops=flops, bytes_accessed=moved, transcendentals=transcendentals)


def whole(shape):
    return pl.BlockSpec(shape, lambda *_: (0,) * len(shape))


def norm(values):
    centred = values - jnp.mean(values, -1, keepdims=True)
    factor = lax.rsqrt(jnp.mean(centred * centred, -1, keepdims=True) + 1e-05)
    return centred * factor, factor


def norm_back(gradient, unit_rows, factor, gain_row):
    scaled = gradient * gain_row
    return factor * (
        scaled
        - jnp.mean(scaled, -1, keepdims=True)
        - unit_rows * jnp.mean(scaled * unit_rows, -1, keepdims=True)
    )


def rotary_tables(rows):
    halfway = HEAD_DIM // 2
    frequency = (1.0 / 10000.0 ** (np.arange(halfway, dtype=np.float32) * 2.0 / HEAD_DIM)).astype(np.float32)
    angles = np.arange(rows, dtype=np.float32)[:, None] * frequency[None, :]
    cosine = np.tile(np.cos(angles), (1, LANES // halfway)).astype(np.float32)
    sine = np.sin(angles)
    sine = np.tile(np.concatenate([-sine, sine], 1), (1, PACK)).astype(np.float32)
    return jnp.asarray(cosine), jnp.asarray(sine)


def swap_halves(values):
    halfway = HEAD_DIM // 2
    lane = lax.broadcasted_iota(jnp.int32, values.shape, 1)
    return jnp.where(
        lane % HEAD_DIM < halfway,
        pltpu.roll(values, LANES - halfway, 1),
        pltpu.roll(values, halfway, 1),
    )


SCALARS = pl.BlockSpec(memory_space=pltpu.SMEM)
LOCAL = pl.BlockSpec(memory_space=pltpu.VMEM)
BESIDE = pl.BlockSpec(memory_space=pl.ANY)


def shaped(shape, dtype=BF):
    return jax.ShapeDtypeStruct(shape, dtype)


def small_call(kernel, place, arrays, out_shape, name, after=()):
    scalars = [] if place is None else [place]

    def body(*refs):
        place_ref, refs = (refs[0], refs[1:]) if scalars else (None, refs)
        kernel(place_ref, refs[: len(arrays)], refs[len(arrays) + len(after) :])

    return pl.pallas_call(
        body,
        in_specs=[SCALARS] * len(scalars) + [LOCAL] * len(arrays) + [BESIDE] * len(after),
        out_specs=[LOCAL] * len(out_shape),
        out_shape=out_shape,
        compiler_params=params(),
        cost_estimate=cost(0, 2 * sum(array.size * array.dtype.itemsize for array in arrays)),
        name=name,
    )(*scalars, *arrays, *after)


def hold(arrays, after):
    count = len(arrays)
    return pl.pallas_call(
        lambda *refs: None,
        in_specs=[BESIDE] * (count + len(after)),
        out_specs=[BESIDE] * count,
        out_shape=[shaped(array.shape, array.dtype) for array in arrays],
        input_output_aliases={index: index for index in range(count)},
        name="hold",
    )(*arrays, *after)


def pick(place, array, parts, after=()):
    micro_total, rows, width = array.shape

    def kernel(place_ref, ins, outs):
        for s in range(parts):
            target = lax.rem(place_ref[1] + s, parts) - place_ref[4]
            outs[s][...] = ins[0][jnp.clip(target, 0, micro_total - 1)]

    return small_call(kernel, place, [array], [shaped((rows, width))] * parts, "pick", after)


def put(place, blocks, micro_total, dtype):
    parts = len(blocks)

    def kernel(place_ref, ins, outs):
        for m in range(micro_total):
            shift = lax.rem(place_ref[1] - place_ref[4] - m + 2 * parts, parts)
            for s in range(parts):

                @pl.when(shift == s)
                def _(m=m, s=s):
                    outs[0][m] = ins[s][...].astype(dtype)

    return small_call(kernel, place, blocks, [shaped((micro_total, *blocks[0].shape), dtype)], "put")[0]


def join(arrays, after=()):
    rows = arrays[0].shape[0]
    columns = sum(array.shape[1] for array in arrays)

    def kernel(place_ref, ins, outs):
        column = 0
        for ref in ins:
            outs[0][:, column : column + ref.shape[1]] = ref[...]
            column += ref.shape[1]

    return small_call(kernel, None, arrays, [shaped((rows, columns))], "join", after)[0]


def of_shift(values, shift):
    found = values[0]
    for s in range(1, len(values)):
        found = jnp.where(shift == s, values[s], found)
    return found


def arrange(place, blocks, widths, after=()):
    parts = len(blocks)
    rows, columns = blocks[0].shape[-2], sum(widths)

    def kernel(place_ref, ins, outs):
        values = [ref[...] for ref in ins]
        for owner in range(parts):
            found = of_shift(values, lax.rem(place_ref[1] - owner + parts, parts))
            column = at = 0
            for index, width in enumerate(widths):
                piece = found[index] if found.ndim == 3 else found[:, column : column + width]
                outs[0][:, at + owner * width : at + (owner + 1) * width] = piece
                column, at = column + width, at + parts * width

    return small_call(kernel, place, blocks, [shaped((rows, parts * columns))], "arrange", after)[0]


def split3(values):
    first = values.astype(BF)
    rest = values - first.astype(F32)
    second = rest.astype(BF)
    return first, second, (rest - second.astype(F32)).astype(BF)


def write_split(ref, begin, values):
    rows = values.shape[0]
    for index, piece in enumerate(split3(values)):
        ref[begin + index * rows : begin + (index + 1) * rows, : values.shape[1]] = piece


def read_split(summed, begin, rows, columns):
    return sum(summed[begin + index * rows : begin + (index + 1) * rows, :columns] for index in range(3))


def sum_refs(refs):
    summed = refs[0][...].astype(F32)
    for ref in refs[1:]:
        summed = summed + ref[...].astype(F32)
    return summed


def cut(summed, place_ref, outs, widths):
    parts, rows = len(outs), summed.shape[0]
    column = at = 0
    for width in widths:
        values = [summed[:, at + owner * width : at + (owner + 1) * width] for owner in range(parts)]
        for s in range(parts):
            outs[s][:rows, column : column + width] = of_shift(values, lax.rem(place_ref[1] + s, parts))
        column, at = column + width, at + parts * width


def deal(place, array, widths, parts):
    rows = array.shape[0]

    def kernel(place_ref, ins, outs):
        cut(ins[0][...], place_ref, outs, widths)

    return small_call(kernel, place, [array], [shaped((rows, sum(widths)))] * parts, "deal")


def by_owner(place, array, widths, parts):
    rows = array.shape[0]

    def kernel(place_ref, ins, outs):
        column = at = 0
        for width in widths:
            for owner in range(parts):
                piece = ins[0][:, at + owner * width : at + (owner + 1) * width]
                outs[0][owner, :, column : column + width] = piece
            column, at = column + width, at + parts * width

    return small_call(kernel, None, [array], [shaped((parts, rows, sum(widths)))], "by_owner")[0]


def total_of(place, blocks, widths):
    rows = blocks[0].shape[0]

    def kernel(place_ref, ins, outs):
        summed = sum_refs(ins)
        column = 0
        for out, width in zip(outs, widths):
            out[...] = summed[:, column : column + width]
            column += width

    return small_call(kernel, place, blocks, [shaped((rows, width), F32) for width in widths], "total_of")


def pair_sums(place, own, received, sums, sums_received):
    count, rows, width = own.shape
    extra = pl.cdiv(3 * sums.shape[0] * sums.shape[1] // width, 16) * 16
    fold = width // sums.shape[1]

    def kernel(place_ref, ins, outs):
        shared = ins[2][...] + ins[3][...]
        depth = shared.shape[0] // fold
        shared = jnp.concatenate([shared[i * depth : (i + 1) * depth, :] for i in range(fold)], 1)
        for index in range(count):
            outs[index][:rows, :] = (ins[0][index].astype(F32) + ins[1][index].astype(F32)).astype(BF)
            outs[index][rows:, :] = jnp.zeros((extra, width), BF)
            write_split(outs[index], rows, shared)

    return small_call(
        kernel, place, [own, received, sums, sums_received], [shaped((rows + extra, width))] * count, "pair_sums"
    )


def plane_sums(place, blocks, widths, parts, rows, sums_shape):
    width, depth = blocks[0].shape[1], sums_shape[0] * sums_shape[1] // blocks[0].shape[1]
    columns = sum(widths)
    fold = width // columns
    extra = pl.cdiv(3 * depth * fold, 16) * 16

    def kernel(place_ref, ins, outs):
        summed = sum_refs(ins)
        shared = read_split(summed, rows, depth, width)
        shared = jnp.concatenate([shared[:, i * columns : (i + 1) * columns] for i in range(fold)], 0)
        cut(summed[:rows, :].astype(BF), place_ref, outs, widths)
        for out in outs:
            out[rows:, :] = jnp.zeros((extra, columns), BF)
            write_split(out, rows, shared)

    return small_call(kernel, place, blocks, [shaped((rows + extra, columns))] * parts, "plane_sums")


def last_sums(place, blocks, widths, rows, shared_rows):
    columns = sum(widths)

    def kernel(place_ref, ins, outs):
        summed = sum_refs(ins)
        column = 0
        for index, width in enumerate(widths):
            outs[0][index] = summed[:rows, column : column + width]
            column += width
        outs[1][...] = read_split(summed, rows, shared_rows, columns)

    shapes = [shaped((len(widths), rows, widths[0]), F32), shaped((shared_rows, columns), F32)]
    return small_call(kernel, place, blocks, shapes, "last_sums")


def first_norm(place, blocks, gain, shift, near):
    parts = len(blocks)
    rows, width = blocks[0].shape

    def kernel(place_ref, ins, outs):
        gain_ref, shift_ref = ins[parts : parts + 2]
        for index, ref in enumerate(ins[parts + 2 :]):
            outs[2][index] = ref[...]
        for s in range(parts):
            here = pl.ds(pl.multiple_of(lax.rem(place_ref[1] - s + parts, parts) * rows, rows), rows)
            x = ins[s][...]
            outs[0][here, :] = x
            unit_rows, _ = norm(x.astype(F32))
            outs[1][here, :] = (unit_rows * gain_ref[...] + shift_ref[...]).astype(BF)

    out_shape = [shaped((parts * rows, width))] * 2 + ([shaped((len(near), *near[0].shape))] if near else [])
    return small_call(kernel, place, [*blocks, gain, shift, *near], out_shape, "first_norm")


def project_kernel(place_ref, normed_ref, bias_ref, cos_ref, sin_ref, *refs, total, pieces):
    weights, (qkv_ref, weight_ref) = refs[:pieces], refs[-2:]
    rows, width = normed_ref.shape
    step = pl.program_id(0)

    @pl.when(step == 0)
    def _():
        if len(weights) == 1:
            weight_ref[...] = weights[0][...]
            return
        half, depth, _ = weights[0].shape
        for index in range(half):
            for odd in range(2):
                owner = jnp.bitwise_xor(place_ref[2], 2 * index + odd)
                weight_ref[pl.ds(pl.multiple_of(owner * depth, depth), depth), :] = weights[odd][index]

    slot = lax.shift_right_logical(jnp.int32(total), place_ref[0])
    normed = normed_ref[...]
    at = pl.ds(pl.multiple_of(lax.rem(step * rows, slot), rows), rows)
    cosine, sine = cos_ref[at, :], sin_ref[at, :]
    for s in range(3):
        rows_out = dot(normed, weight_ref[:, s * width : (s + 1) * width])
        rows_out = rows_out + bias_ref[:, s * width : (s + 1) * width]
        if s == 2:
            qkv_ref[:, s * width : (s + 1) * width] = rows_out.astype(BF)
            continue
        for tile in range(width // LANES):
            piece = rows_out[:, tile * LANES : (tile + 1) * LANES]
            piece = piece * cosine + swap_halves(piece) * sine
            if s == 0:
                piece = piece * HEAD_DIM ** (-0.5)
            column = s * width + tile * LANES
            qkv_ref[:, column : column + LANES] = piece.astype(BF)


def project(place, normed, weights, bias, cosine, sine, after=()):
    total, width = normed.shape
    return pl.pallas_call(
        functools.partial(project_kernel, total=total, pieces=len(weights)),
        grid=(total // BLOCK,),
        in_specs=[
            SCALARS,
            pl.BlockSpec((BLOCK, width), lambda i: (i, 0)),
            whole((1, 3 * width)),
            whole((total, LANES)),
            whole((total, LANES)),
        ]
        + [whole(weight.shape) for weight in weights]
        + [BESIDE] * len(after),
        out_specs=[pl.BlockSpec((BLOCK, 3 * width), lambda i: (i, 0)), whole((width, 3 * width))],
        out_shape=[shaped((total, 3 * width)), shaped((width, 3 * width))],
        compiler_params=params(),
        cost_estimate=cost(6 * total * width * width, 12 * total * width),
        name="project",
    )(place, normed, bias, cosine, sine, *weights, *after)


def by_bucket(place_ref, total, lens_ref, body):
    bucket, micro = place_ref[0], place_ref[3]
    for code in range(3):
        count = 1 << code
        width = total // count
        step = 4 // count

        @pl.when(bucket == code)
        def _(count=count, width=width, step=step):
            if count == 1:
                body(0, width, lens_ref[micro, 0])
            else:

                @pl.loop(0, count)
                def _(index):
                    body(pl.multiple_of(index * width, width), width, lens_ref[micro, step * index])


def attend_kernel(place_ref, lens_ref, q_ref, k_ref, v_ref, out_ref, log_ref):
    total = q_ref.shape[0]
    lane = lax.broadcasted_iota(jnp.int32, (1, LANES), 1)
    area = lane // HEAD_DIM
    sub = lane % HEAD_DIM

    def sequence(first, width, length):
        keys, values = k_ref[pl.ds(first, width), :], v_ref[pl.ds(first, width), :]
        position = lax.broadcasted_iota(jnp.int32, (width, 1), 0)
        hidden = jnp.where(position < length, 0.0, -1e30).astype(BF)
        for start in range(0, width, BLOCK):
            here = pl.ds(first + start, BLOCK)
            queries = q_ref[here, :]
            total_rows, highs = None, []
            for head in range(PACK):
                own = area == head
                extra = (area == (head + 1) % PACK) & (sub == 0)
                q_one = jnp.where(own, queries, jnp.where(extra, BF(1), BF(0)))
                k_one = jnp.where(extra, jnp.broadcast_to(hidden, keys.shape), keys)
                scores = dot(q_one, k_one, NT)
                high = jnp.max(scores, 1, keepdims=True)
                weights = jnp.exp(scores - high).astype(BF)
                v_one = jnp.concatenate(
                    [
                        jnp.where(own, values, BF(0)),
                        jnp.broadcast_to(jnp.where(own, BF(1), BF(0)), values.shape),
                    ],
                    1,
                )
                term = dot(weights, v_one)
                total_rows = term if total_rows is None else total_rows + term
                highs.append(high)
            high = highs[PACK - 1]
            for head in range(PACK - 1):
                high = jnp.where(area == head, highs[head], high)
            summed = total_rows[:, LANES:]
            out_ref[here, :] = (total_rows[:, :LANES] / summed).astype(BF)
            log_ref[here, :] = high + jnp.log(summed)

    by_bucket(place_ref, total, lens_ref, sequence)


def attend(place, lens, qkv):
    total = qkv.shape[0]
    tiles = qkv.shape[1] // 3 // LANES
    scalar = pl.BlockSpec(memory_space=pltpu.SMEM)

    def tile(which):
        return pl.BlockSpec((total, LANES), lambda j: (0, which * tiles + j))

    return pl.pallas_call(
        attend_kernel,
        grid=(tiles,),
        in_specs=[scalar, scalar, tile(0), tile(1), tile(2)],
        out_specs=[tile(0), tile(0)],
        out_shape=[
            jax.ShapeDtypeStruct((total, tiles * LANES), BF),
            jax.ShapeDtypeStruct((total, tiles * LANES), F32),
        ],
        compiler_params=params(),
        cost_estimate=cost(
            12 * tiles * PACK * total * total * 256, 12 * total * tiles * LANES, tiles * PACK * total * total
        ),
        name="attend",
    )(place, lens, qkv, qkv, qkv)


def attend_back_kernel(
    place_ref, lens_ref, q_ref, k_ref, v_ref, out_ref, grad_ref, log_ref, cos_ref, sin_ref,
    dq_ref, dk_ref, dv_ref, q_extra, g_extra, dq_total, dk_total,
):
    total = q_ref.shape[0]
    lane = lax.broadcasted_iota(jnp.int32, (1, LANES), 1)
    area = lane // HEAD_DIM
    sub = lane % HEAD_DIM
    first, second, third = split3(-pltpu.roll(log_ref[...], HEAD_DIM, 1))
    q_extra[...] = jnp.where(
        sub == 0, first, jnp.where(sub == 1, second, jnp.where(sub == 2, third, jnp.where(sub == 3, BF(1), BF(0))))
    )
    product = grad_ref[...].astype(F32) * out_ref[...].astype(F32)
    row_area = lax.broadcasted_iota(jnp.int32, (LANES, LANES), 0) // HEAD_DIM
    column_area = lax.broadcasted_iota(jnp.int32, (LANES, LANES), 1) // HEAD_DIM
    spread = jnp.where((row_area + 1) % PACK == column_area, 1.0, 0.0).astype(BF)
    delta = sum(dot(piece, spread) for piece in split3(product))
    first, second, third = split3(-delta)
    g_extra[...] = jnp.where(sub == 0, first, jnp.where(sub == 1, second, jnp.where(sub == 2, third, BF(0))))

    def sequence(begin, width, length):
        keys, values = k_ref[pl.ds(begin, width), :], v_ref[pl.ds(begin, width), :]
        position = lax.broadcasted_iota(jnp.int32, (width, 1), 0)
        hidden = jnp.where(position < length, 0.0, -1e30).astype(BF)
        k_extra = jnp.where(
            sub < 3, BF(1), jnp.where(sub == 3, jnp.broadcast_to(hidden, keys.shape), BF(0))
        )
        v_extra = jnp.broadcast_to(jnp.where(sub < 3, BF(1), BF(0)), values.shape)
        dv = jnp.zeros((width, LANES), F32)
        dk = jnp.zeros((width, LANES), F32)
        for start in range(0, width, BLOCK):
            here = pl.ds(begin + start, BLOCK)
            queries, grads = q_ref[here, :], grad_ref[here, :]
            q_more, g_more = q_extra[here, :], g_extra[here, :]
            dq = None
            for head in range(PACK):
                own, after = area == head, area == (head + 1) % PACK
                q_own, g_own = jnp.where(own, queries, BF(0)), jnp.where(own, grads, BF(0))
                k_one, v_one = jnp.where(own, keys, k_extra), jnp.where(own, values, v_extra)
                prob = jnp.exp(dot(k_one, jnp.where(after, q_more, q_own), NT))
                grad_prob = dot(v_one, jnp.where(after, g_more, g_own), NT)
                grad_scores = (prob * grad_prob).astype(BF)
                dv = dv + dot(prob.astype(BF), g_own)
                dk = dk + dot(grad_scores, q_own)
                term = dot(jnp.where(own, keys, BF(0)), grad_scores, TN)
                dq = term if dq is None else dq + term
            dq_total[here, :] = dq.T
        dv_ref[pl.ds(begin, width), :] = dv.astype(BF)
        dk_total[pl.ds(begin, width), :] = dk

    by_bucket(place_ref, total, lens_ref, sequence)
    slot = lax.shift_right_logical(jnp.int32(total), place_ref[0])
    for start in range(0, total, BLOCK):
        here = pl.ds(start, BLOCK)
        at = pl.ds(pl.multiple_of(lax.rem(jnp.int32(start), slot), BLOCK), BLOCK)
        cosine, sine = cos_ref[at, :], sin_ref[at, :]
        dq, dk = dq_total[here, :], dk_total[here, :]
        dq_ref[here, :] = ((dq * cosine - swap_halves(dq) * sine) * HEAD_DIM ** (-0.5)).astype(BF)
        dk_ref[here, :] = (dk * cosine - swap_halves(dk) * sine).astype(BF)


def attend_back(place, lens, qkv, attended, grad, log_total, cosine, sine):
    total = qkv.shape[0]
    tiles = qkv.shape[1] // 3 // LANES
    scalar = pl.BlockSpec(memory_space=pltpu.SMEM)

    def tile(which):
        return pl.BlockSpec((total, LANES), lambda j: (0, which * tiles + j))

    return pl.pallas_call(
        attend_back_kernel,
        grid=(tiles,),
        in_specs=[scalar, scalar, tile(0), tile(1), tile(2), tile(0), tile(0), tile(0)]
        + [whole((total, LANES))] * 2,
        out_specs=[tile(0)] * 3,
        out_shape=[jax.ShapeDtypeStruct((total, tiles * LANES), BF)] * 3,
        scratch_shapes=[pltpu.VMEM((total, LANES), BF)] * 2 + [pltpu.VMEM((total, LANES), F32)] * 2,
        compiler_params=params(),
        cost_estimate=cost(
            24 * tiles * PACK * total * total * 256, 20 * total * tiles * LANES, tiles * PACK * total * total
        ),
        name="attend_back",
    )(place, lens, qkv, qkv, qkv, attended, grad, log_total, cosine, sine)


def column_sums(values):
    return jnp.sum(values, 0, keepdims=True)


def row_weights(place_ref, lens_ref, masked_ref, total, groups_ratio=3.0 / 8.0):
    micro = place_ref[3]
    row = lax.broadcasted_iota(jnp.int32, (1, total), 1)
    slot = lax.shift_right_logical(jnp.int32(total), place_ref[0])
    position = jnp.bitwise_and(row, slot - 1)
    begin = row - position
    length = jnp.zeros((1, total), jnp.int32)
    for index in range(4):
        length = jnp.where(begin == index * (total // 4), lens_ref[micro, index], length)
    chosen = masked_ref[pl.ds(micro, 1), :]
    counted = jnp.where((position < length) & (place_ref[5] == 1), chosen, 0).astype(F32)
    weights = counted * (groups_ratio * total / jnp.maximum(jnp.sum(counted), 1.0))
    return jnp.broadcast_to(weights, (LANES, total)).T


def feed_kernel(
    place_ref, lens_ref, masked_ref, x_ref, att_ref, gain_ref, shift_ref, out_bias_ref, up_bias_ref, down_bias_ref,
    *refs, row_steps, chunks, pieces,
):
    pieces_refs, refs = refs[:pieces], refs[pieces:]
    grad_refs, layer_refs = refs[:row_steps], refs[row_steps : 2 * row_steps]
    residual_ref, grad_att_ref, sums_ref, grads_ref = refs[2 * row_steps : 2 * row_steps + 4]
    normed, tops, mixes, atts, hidden, ups, weights, grad_rows, layer_rows, *held = refs[2 * row_steps + 4 :]
    step = pl.program_id(0)
    rows, width = x_ref.shape
    table = held[0] if held else pieces_refs[0]
    up_ref, down_ref = table.at[:, : chunks * width], table.at[:, chunks * width : 2 * chunks * width]
    mix_ref = table.at[:, 2 * chunks * width :]

    @pl.when(step == 0)
    def _():
        if held:
            blocks, parts, depth, _ = pieces_refs[0].shape
            share, mix_share = width * chunks // parts, width // parts
            for block in range(blocks):
                rows_at = slice(block * depth, (block + 1) * depth)
                for part in range(parts):
                    found = pieces_refs[0][block, part]
                    up_ref[rows_at, part * share : (part + 1) * share] = found[:, :share]
                    down_ref[rows_at, part * share : (part + 1) * share] = found[:, share : 2 * share]
                    mix_ref[rows_at, part * mix_share : (part + 1) * mix_share] = found[:, 2 * share :]
        sums_ref[...] = jnp.zeros_like(sums_ref)
        weights[...] = row_weights(place_ref, lens_ref, masked_ref, rows * row_steps)

    for s in range(row_steps):

        @pl.when((step < row_steps) & (lax.rem(place_ref[1] - step + 2 * row_steps, row_steps) == s))
        def _(s=s):
            grad_rows[...] = grad_refs[s][...]

    @pl.when(step < row_steps)
    def _():
        here = pl.ds(pl.multiple_of(step * rows, rows), rows)
        attended = att_ref[...]
        residual = x_ref[...].astype(F32) + dot(attended, mix_ref[...], NT) + out_bias_ref[...]
        unit_rows, factor = norm(residual)
        gain = gain_ref[...]
        second = (unit_rows * gain + shift_ref[...]).astype(BF)
        weight = weights[here, :]
        top = grad_rows[...].astype(F32) * jnp.concatenate([weight] * (width // LANES), 1)
        top_low = top.astype(BF)
        normed[here, :] = second
        tops[here, :] = top_low
        atts[here, :] = attended
        below = jnp.zeros((rows, width), F32)
        grad_second = jnp.zeros((rows, width), F32)
        for chunk in range(chunks):
            columns = slice(chunk * width, (chunk + 1) * width)
            up_weight, down_weight = up_ref[:, columns], down_ref[:, columns]
            up = dot(second, up_weight) + up_bias_ref[:, columns]
            share = 0.5 * (1.0 + lax.erf(up * 0.7071067811865476))
            slope = share + up * jnp.exp(-0.5 * up * up) * 0.3989422804014327
            low = (up * share).astype(BF)
            hidden[here, columns] = low
            below = below + dot(low, down_weight, NT)
            grad_up = (dot(top_low, down_weight) * slope).astype(BF)
            ups[here, columns] = grad_up
            sums_ref[4 + chunk : 5 + chunk, :] += column_sums(grad_up.astype(F32))
            grad_second = grad_second + dot(grad_up, up_weight, NT)
        layer_rows[...] = (residual + below + down_bias_ref[...]).astype(BF)
        grad_residual = top + norm_back(grad_second, unit_rows, factor, gain)
        residual_ref[...] = grad_residual
        mixed = grad_residual.astype(BF)
        mixes[here, :] = mixed
        grad_att_ref[...] = dot(mixed, mix_ref[...]).astype(BF)
        sums_ref[0:1, :] += column_sums(grad_second * unit_rows)
        sums_ref[1:2, :] += column_sums(grad_second)
        sums_ref[2:3, :] += column_sums(grad_residual)
        sums_ref[3:4, :] += column_sums(top)

    for s in range(row_steps):

        @pl.when((step < row_steps) & (lax.rem(step - place_ref[1] + row_steps, row_steps) == s))
        def _(s=s):
            layer_refs[s][...] = layer_rows[...]

    for chunk in range(chunks):
        columns = slice(chunk * width, (chunk + 1) * width)

        @pl.when(step == row_steps + chunk)
        def _(columns=columns):
            grads_ref[...] = dot(normed[...], ups[:, columns], TN).astype(BF)

        @pl.when(step == row_steps + chunks + chunk)
        def _(columns=columns):
            grads_ref[...] = dot(tops[...], hidden[:, columns], TN).astype(BF)

    @pl.when(step == row_steps + 2 * chunks)
    def _():
        grads_ref[...] = dot(mixes[...], atts[...], TN).astype(BF)


def feed(place, lens, masked, x, attended, grad_blocks, gain, shift, out_bias, up_bias, down_bias, weights):
    total, width = x.shape
    parts, rows = len(grad_blocks), grad_blocks[0].shape[0]
    hidden_width = up_bias.shape[1]
    chunks = hidden_width // width
    row = pl.BlockSpec((rows, width), lambda i: (jnp.minimum(i, parts - 1), 0))
    once = pl.Buffered(1)
    return pl.pallas_call(
        functools.partial(feed_kernel, row_steps=parts, chunks=chunks, pieces=len(weights)),
        grid=(parts + 2 * chunks + 1,),
        in_specs=[
            SCALARS,
            SCALARS,
            whole(masked.shape),
            row,
            row,
            whole((1, width)),
            whole((1, width)),
            whole((1, width)),
            whole((1, hidden_width)),
            whole((1, width)),
        ]
        + [pl.BlockSpec(weight.shape, lambda i, dims=weight.ndim: (0,) * dims, pipeline_mode=once) for weight in weights]
        + [pl.BlockSpec((rows, width), lambda i: (0, 0), pipeline_mode=once)] * parts,
        out_specs=[whole((rows, width))] * parts
        + [row, row, whole((16, width)), pl.BlockSpec((width, width), lambda i: (0, jnp.maximum(i - parts, 0)))],
        out_shape=[shaped((rows, width))] * parts
        + [
            shaped((total, width), F32),
            shaped((total, width)),
            shaped((16, width), F32),
            shaped((width, (2 * chunks + 1) * width)),
        ],
        scratch_shapes=[pltpu.VMEM((total, width), BF)] * 4
        + [pltpu.VMEM((total, hidden_width), BF)] * 2
        + [pltpu.VMEM((total, LANES), F32)]
        + [pltpu.VMEM((rows, width), BF)] * 2
        + ([pltpu.VMEM((width, 2 * hidden_width + width), BF)] if weights[0].ndim == 4 else []),
        compiler_params=params(),
        cost_estimate=cost(6 * total * width * width * (2 * chunks + 1), 24 * width * hidden_width),
        name="feed",
    )(place, lens, masked, x, attended, gain, shift, out_bias, up_bias, down_bias, *weights, *grad_blocks)


def project_grads_kernel(place_ref, normed_ref, q_ref, k_ref, v_ref, *refs, pieces, skip):
    outs, sums_ref = refs[skip:-1], refs[-1]
    depth = normed_ref.shape[1] // pieces
    for s, ref in enumerate((q_ref, k_ref, v_ref)):

        @pl.when(pl.program_id(0) == s)
        def _(s=s, ref=ref):
            grads = ref[...]
            found = dot(normed_ref[...], grads, TN).astype(BF)
            sums_ref[s : s + 1, :] = column_sums(grads.astype(F32))
            if pieces == 1:
                outs[0][...] = found
                return
            for piece in range(pieces):
                block = found[piece * depth : (piece + 1) * depth, :]
                offset = jnp.bitwise_xor(place_ref[2], piece)
                for odd in range(2):

                    @pl.when(lax.rem(offset, 2) == odd)
                    def _(odd=odd, block=block, offset=offset):
                        outs[odd][lax.shift_right_logical(offset, 1)] = block


def project_grads(place, normed, grads, pieces, after):
    total, width = normed.shape
    if pieces == 1:
        outs = [pl.BlockSpec((width, width), lambda i: (0, i))]
        shapes = [jax.ShapeDtypeStruct((width, 3 * width), BF)]
    else:
        half, depth = pieces // 2, width // pieces
        outs = [pl.BlockSpec((half, depth, width), lambda i: (0, 0, i))] * 2
        shapes = [jax.ShapeDtypeStruct((half, depth, 3 * width), BF)] * 2
    return pl.pallas_call(
        functools.partial(project_grads_kernel, pieces=pieces, skip=len(after)),
        grid=(3,),
        in_specs=[SCALARS] + [whole((total, width))] * 4 + [BESIDE] * len(after),
        out_specs=outs + [whole((8, width))],
        out_shape=shapes + [jax.ShapeDtypeStruct((8, width), F32)],
        compiler_params=params(),
        cost_estimate=cost(6 * total * width * width, 14 * total * width),
        name="project_grads",
    )(place, normed, *grads, *after)


def project_back_kernel(place_ref, q_ref, k_ref, v_ref, weight_ref, x_ref, residual_ref, gain_ref, *refs, parts):
    outs, sums_ref, found = refs[:parts], refs[parts], refs[parts + 1]
    width = x_ref.shape[1]
    step = pl.program_id(0)

    @pl.when(step == 0)
    def _():
        sums_ref[...] = jnp.zeros_like(sums_ref)

    grad_first = sum(
        dot(ref[...], weight_ref[:, s * width : (s + 1) * width], NT) for s, ref in enumerate((q_ref, k_ref, v_ref))
    )
    unit_rows, factor = norm(x_ref[...].astype(F32))
    found[...] = (residual_ref[...] + norm_back(grad_first, unit_rows, factor, gain_ref[...])).astype(BF)
    sums_ref[0:1, :] += column_sums(grad_first * unit_rows)
    sums_ref[1:2, :] += column_sums(grad_first)
    for s in range(parts):

        @pl.when(lax.rem(step - place_ref[1] + parts, parts) == s)
        def _(s=s):
            outs[s][...] = found[...]


def project_back(place, grads, weight, x, grad_residual, gain, parts):
    total, width = x.shape
    rows = total // parts
    row = pl.BlockSpec((rows, width), lambda i: (i, 0))
    return pl.pallas_call(
        functools.partial(project_back_kernel, parts=parts),
        grid=(parts,),
        in_specs=[SCALARS, row, row, row, whole((width, 3 * width)), row, row, whole((1, width))],
        out_specs=[whole((rows, width))] * parts + [whole((8, width))],
        out_shape=[shaped((rows, width))] * parts + [shaped((8, width), F32)],
        scratch_shapes=[pltpu.VMEM((rows, width), BF)],
        compiler_params=params(),
        cost_estimate=cost(6 * total * width * width, 16 * total * width),
        name="project_back",
    )(place, *grads, weight, x, grad_residual, gain)


def shards(
    inputs,
    grad_out,
    masked,
    bucket,
    lengths,
    first_gain,
    first_shift,
    second_gain,
    second_shift,
    qkv_weight,
    qkv_bias,
    out_weight,
    out_bias,
    up_weight,
    up_bias,
    down_weight,
    down_bias,
):
    parts = lax.axis_size("tensor")
    dp_parts = lax.axis_size("dp")
    here = lax.axis_index("tensor")
    dp_here = lax.axis_index("dp")
    micro_total, rows, width = inputs.shape
    total = rows * parts
    assert micro_total <= parts
    spare = parts - micro_total
    first = (dp_here % 2) * spare
    micro = here - first
    working = (micro >= 0) & (micro < micro_total)
    micro_at = jnp.clip(micro, 0, micro_total - 1)

    def pairs(shift, towards):
        out = []
        for r in range(dp_parts):
            for t in range(parts):
                u = (t + shift) % parts
                owner = (u if towards else t) - (r % 2) * spare
                if 0 <= owner < micro_total:
                    out.append((r * parts + t, r * parts + u))
        return out

    def to_owners(blocks):
        return [blocks[0]] + [
            lax.ppermute(blocks[shift], ("dp", "tensor"), pairs(shift, True)) for shift in range(1, parts)
        ]

    def from_owners(blocks):
        return [blocks[0]] + [
            lax.ppermute(blocks[shift], ("dp", "tensor"), pairs(shift, False)) for shift in range(1, parts)
        ]

    def shift_by(array, shift):
        return lax.ppermute(array, "tensor", [(t, (t + shift) % parts) for t in range(parts)])

    def swap_by(array, bits):
        return lax.ppermute(array, "dp", [(r, r ^ bits) for r in range(dp_parts)])

    rows_w, cols_ffn, cols_attn = qkv_weight.shape[1], up_weight.shape[1], out_weight.shape[1]
    pieces = dp_parts if dp_parts == 8 else 1
    code = jnp.where(working, lax.dynamic_index_in_dim(bucket, micro_at, 0, False)[0], 2)
    place = jnp.stack([code, here, dp_here, micro_at, first, working]).astype(jnp.int32)

    attn = [qkv_weight] + [shift_by(qkv_weight, shift) for shift in range(1, parts)]
    blocks = to_owners(pick(place, inputs, parts, attn[1:2]))
    attn = arrange(place, attn, (cols_attn,) * 3)
    cosine, sine = rotary_tables(total)
    rest = lax.all_gather(join([up_weight, down_weight, out_weight]), ("dp", "tensor"), axis=0)
    rest = rest.reshape(dp_parts, parts, rows_w, -1)
    if pieces == 1:
        rest = rest.transpose(0, 2, 1, 3).reshape(width, parts, -1)
        rest = jnp.split(rest, (cols_ffn, 2 * cols_ffn), 2)
        rest = jnp.concatenate([piece.reshape(width, -1) for piece in rest], 1)
        attn = [lax.all_gather(attn, "dp", axis=0, tiled=True)]
        x, first_normed = first_norm(place, blocks, first_gain[None], first_shift[None], [])
    else:
        near = [attn] + [swap_by(attn, bits) for bits in range(2, pieces, 2)]
        x, first_normed, near = first_norm(place, blocks, first_gain[None], first_shift[None], near)
        attn = [near, swap_by(near, 1)]
    qkv, attn = project(place, first_normed, attn, qkv_bias.reshape(1, -1), cosine, sine)
    grad_blocks = to_owners(pick(place, grad_out, parts, (qkv,)))
    attended, log_total = attend(place, lengths, qkv)
    *layer, grad_residual, grad_attended, feed_sums, feed_grads = feed(
        place, lengths, masked, x, attended, grad_blocks, second_gain[None], second_shift[None],
        out_bias[None], up_bias[None], down_bias[None], [rest],
    )
    layer_out = put(place, from_owners(layer), micro_total, BF)
    feed_grads = lax.psum_scatter(feed_grads, "dp", scatter_dimension=0, tiled=True)
    feed_grads = by_owner(place, feed_grads, (cols_ffn, cols_ffn, cols_attn), parts)
    feed_grads = lax.psum_scatter(feed_grads, "tensor", scatter_dimension=0, tiled=False)
    grad_up, grad_down, grad_mix = total_of(place, [feed_grads], (cols_ffn, cols_ffn, cols_attn))
    grads = attend_back(place, lengths, qkv, attended, grad_attended, log_total, cosine, sine)
    *attn_grads, bias_sums = project_grads(place, first_normed, grads, pieces, (layer_out,))
    *grad_in, first_sums = project_back(place, grads, attn, x, grad_residual, first_gain[None], parts)
    grad_inputs = put(place, from_owners(grad_in), micro_total, F32)
    chunks = up_bias.shape[0] // width
    sums = jnp.concatenate([feed_sums[: 4 + chunks], bias_sums[:3], first_sums[:2]])
    sums = jnp.pad(sums, ((0, -sums.shape[0] % 3), (0, 0)))
    if pieces == 1:
        attn_grads = lax.psum_scatter(attn_grads[0], "dp", scatter_dimension=0, tiled=True)
        attn_grads = deal(place, attn_grads, (cols_attn,) * 3, parts)
        attn_grads = [attn_grads[0]] + [shift_by(attn_grads[shift], shift) for shift in range(1, parts)]
        attn_grads = jnp.stack(total_of(place, attn_grads, (cols_attn,) * 3))
        sums = jnp.sum(lax.all_gather(sums, ("dp", "tensor"), axis=0), 0)
    else:
        even, odd = attn_grads
        both = pair_sums(place, even, swap_by(odd, 1), sums, swap_by(sums, 1))
        both = [both[0]] + [swap_by(both[index], 2 * index) for index in range(1, pieces // 2)]
        dealt = plane_sums(place, both, (cols_attn,) * 3, parts, rows_w, sums.shape)
        dealt = [dealt[0]] + [shift_by(dealt[shift], shift) for shift in range(1, parts)]
        shared_rows = sums.size // (3 * cols_attn)
        attn_grads, shared = last_sums(place, dealt, (cols_attn,) * 3, rows_w, shared_rows)
        fold = 3 * width // (3 * cols_attn)
        shared = jnp.concatenate(jnp.split(shared, fold, 0), 1)
        sums = jnp.concatenate(jnp.split(shared, 3, 1), 0)
    feed_sums, late_sums = sums[: 4 + chunks], sums[4 + chunks :]
    return (
        layer_out,
        grad_inputs,
        attn_grads,
        grad_mix,
        grad_up,
        grad_down,
        late_sums[3],
        late_sums[4],
        feed_sums[0],
        feed_sums[1],
        late_sums[:3],
        feed_sums[2],
        feed_sums[4:].reshape(-1),
        feed_sums[3],
    )


def solution(mesh):
    placed = (
        P(None, ("dp", "tensor"), None),
        P(None, ("dp", "tensor"), None),
        P(None, "dp"),
        P(None, "dp"),
        P(None, "dp"),
        P(),
        P(),
        P(),
        P(),
        P(None, "dp", "tensor"),
        P(),
        P("dp", "tensor"),
        P(),
        P("dp", "tensor"),
        P(),
        P("dp", "tensor"),
        P(),
    )
    return jax.shard_map(
        shards,
        mesh=mesh,
        in_specs=placed,
        out_specs=(
            P(None, ("dp", "tensor"), None),
            P(None, ("dp", "tensor"), None),
            P(None, "dp", "tensor"),
            P("dp", "tensor"),
            P("dp", "tensor"),
            P("dp", "tensor"),
            P(),
            P(),
            P(),
            P(),
            P(),
            P(),
            P(),
            P(),
        ),
        check_vma=False,
    )
```
